32 devices in a mesh: sample: 8 (over z, y), span: 2 (over x), kvhead: 2 (over core).
Axes of the slice: x: 2, y: 2, z: 4, core: 2. Of those that a mesh axis runs over, the one named last changes fastest.
Arguments:
- queries: bfloat16 [8, 256, 3584], P('sample', None, 'kvhead'), may hold values from -6 to 6
- outputs: bfloat16 [8, 256, 3584], P('sample', None, 'kvhead'), may hold values from -6 to 6
- grad_out: bfloat16 [8, 256, 3584], P('sample', None, 'kvhead'), may hold values from -48 to 48
- log_norms: float32 [8, 28, 256], P('sample', 'kvhead'), as said below
- lengths: int32 [8], P('sample'), may hold values from 1 to 256, 512 in all
- prompt_key_rows: bfloat16 [2048, 512], P(('sample', 'span'), 'kvhead'), may hold values from -9 to 9
- prompt_value_rows: bfloat16 [2048, 512], P(('sample', 'span'), 'kvhead'), may hold values from -6 to 6
- slice_key_rows: bfloat16 [8, 256, 512], P('sample', 'span', 'kvhead'), may hold values from -9 to 9
- slice_value_rows: bfloat16 [8, 256, 512], P('sample', 'span', 'kvhead'), may hold values from -6 to 6
Outputs:
- grad_queries: bfloat16 [8, 256, 3584], P('sample', 'span', 'kvhead')
- grad_k_prompt: bfloat16 [2048, 512], P(('sample', 'span'), 'kvhead')
- grad_v_prompt: bfloat16 [2048, 512], P(('sample', 'span'), 'kvhead')
- grad_k_self: bfloat16 [8, 256, 512], P('sample', 'span', 'kvhead')
- grad_v_self: bfloat16 [8, 256, 512], P('sample', 'span', 'kvhead')
The draws below stay inside these ranges and needn't reach their ends.
Inputs may be any that keep to these rules, and one draw needn't show every extreme that they name: `log_norms`: every entry lies between 0.8 and 2.4 above the natural logarithm of 2304.
All inputs are finite; a program needn't handle non-finite values. No bound on the sum of `lengths` on one device may be relied on, other than what follows from the above.
Results may differ from the reference program's by a relative error of at most 0.0051.
Values may be sent and summed in bfloat16 or wider, within the bound.
A program may use at most 64 MiB of HBM per device.

```python
import math
import jax
import jax.numpy as jnp
import numpy as np
from jax import lax

QUERY_HEADS = 28
KEY_VALUE_HEADS = 4
HEAD_WIDTH = 128
SLICE_LENGTH = 256
SAMPLE_COUNT = 8
PROMPT_LENGTH = 2048


def draw_log_norms(key, part):
    base_level = math.log(PROMPT_LENGTH + SLICE_LENGTH) + 1.1
    offsets = jax.random.uniform(key, (SAMPLE_COUNT, QUERY_HEADS, SLICE_LENGTH), jnp.float32, 0.0, 1.0)
    return (base_level + offsets).astype(jnp.float32)


def block_scale(own_key, extent, pieces, smallest, largest):
    gain, own = 1.0, jax.random.fold_in(own_key, 6)
    for dim, shards_of in pieces:
        steps = jnp.exp(jax.random.uniform(jax.random.fold_in(own, dim), (shards_of,), jnp.float32, smallest / len(pieces), largest / len(pieces)))
        gain = gain * jnp.repeat(steps, extent[dim] // shards_of).reshape([-1 if axis == dim else 1 for axis in range(len(extent))])
    return gain


def length_profile(number_of, total, reach, slope):
    loads = [(1 << 20) // math.isqrt(grade ** slope) + 1 for grade in range(2, number_of + 1)]
    spare, given = total - reach - (number_of - 1), [1] * (number_of - 1)
    while spare > 0:
        free = [i for i in range(number_of - 1) if given[i] < reach]
        mass, budget = sum([loads[i] for i in free]), spare
        for i in free:
            addition = min(reach - given[i], max(1, budget * loads[i] // mass), spare)
            given[i] = given[i] + addition
            spare = spare - addition
    return np.array([reach] + given)


def uneven(own_key, count, total, limit, skew):
    if count == 2:
        one = jax.random.randint(own_key, (), max(1, total - limit), min(limit, total - 1) + 1)
        return jnp.stack([one, total - one])
    sizes = jnp.asarray(length_profile(count, total, limit, skew), jnp.int32)
    twos = (count - 1) // 2
    source_of, taker = sizes[1:1 + 2 * twos:2], sizes[2:2 + 2 * twos:2]
    slack = jnp.minimum(source_of - 1, limit - taker)
    passed = jax.random.randint(jax.random.fold_in(own_key, 1), (twos,), 0, 1 << 20) % (slack + 1)
    sizes = sizes.at[1:1 + 2 * twos:2].set(source_of - passed).at[2:2 + 2 * twos:2].set(taker + passed)
    return sizes[jax.random.permutation(jax.random.fold_in(own_key, 2), count)]


def centred(key, extent, spread, limit, split=(), dtype=jnp.bfloat16):
    loudness = block_scale(key, extent, split, -0.22, 0.18) if split else 1.0
    values = jax.random.normal(key, extent, jnp.float32) * spread * loudness
    return jnp.minimum(jnp.maximum(values, -limit), limit).astype(dtype)


def setup_inputs(seed: int = 0) -> dict:
    key_of = jax.random.split(jax.random.key(seed), 10)
    queries = centred(key_of[0], (SAMPLE_COUNT, SLICE_LENGTH, QUERY_HEADS * HEAD_WIDTH), 1.0, 6.0, ((0, 8), (2, 2)))
    outputs = centred(key_of[1], (SAMPLE_COUNT, SLICE_LENGTH, QUERY_HEADS * HEAD_WIDTH), 1.0, 6.0, ((0, 8), (2, 2)))
    grad_out = centred(key_of[2], (SAMPLE_COUNT, SLICE_LENGTH, QUERY_HEADS * HEAD_WIDTH), 8.0, 48.0, ((0, 8), (2, 2)))
    log_norms = draw_log_norms(jax.random.fold_in(key_of[9], 71), 0)
    lengths = uneven(key_of[4], SAMPLE_COUNT, SAMPLE_COUNT * SLICE_LENGTH // 4, SLICE_LENGTH, 2).astype(jnp.int32)
    prompt_key_rows = centred(key_of[5], (PROMPT_LENGTH, KEY_VALUE_HEADS * HEAD_WIDTH), 1.5, 9.0, ((0, 16), (1, 2)))
    prompt_value_rows = centred(key_of[6], (PROMPT_LENGTH, KEY_VALUE_HEADS * HEAD_WIDTH), 1.0, 6.0, ((0, 16), (1, 2)))
    slice_key_rows = centred(key_of[7], (SAMPLE_COUNT, SLICE_LENGTH, KEY_VALUE_HEADS * HEAD_WIDTH), 1.5, 9.0, ((0, 8), (1, 2), (2, 2)))
    slice_value_rows = centred(key_of[8], (SAMPLE_COUNT, SLICE_LENGTH, KEY_VALUE_HEADS * HEAD_WIDTH), 1.0, 6.0, ((0, 8), (1, 2), (2, 2)))
    return {"queries": queries, "outputs": outputs, "grad_out": grad_out, "log_norms": log_norms, "lengths": lengths, "prompt_key_rows": prompt_key_rows, "prompt_value_rows": prompt_value_rows, "slice_key_rows": slice_key_rows, "slice_value_rows": slice_value_rows}


def divide_heads(matrix, head_count):
    return matrix.reshape(matrix.shape[0], head_count, HEAD_WIDTH).transpose(1, 0, 2)

def join_heads(blocks):
    return blocks.transpose(1, 0, 2).reshape(blocks.shape[1], blocks.shape[0] * HEAD_WIDTH)

def reference(queries, outputs, grad_out, log_norms, lengths, prompt_key_rows, prompt_value_rows, slice_key_rows, slice_value_rows):
    query_group_width = QUERY_HEADS // KEY_VALUE_HEADS
    score_scale = 1.0 / math.sqrt(HEAD_WIDTH)
    expanded_key_heads = divide_heads(prompt_key_rows, KEY_VALUE_HEADS)
    expanded_value_heads = divide_heads(prompt_value_rows, KEY_VALUE_HEADS)
    row_pos = lax.broadcasted_iota(jnp.int32, (query_group_width * SLICE_LENGTH,), 0) % SLICE_LENGTH
    col_pos = lax.broadcasted_iota(jnp.int32, (SLICE_LENGTH,), 0)
    visible_mask = col_pos[None, :] <= row_pos[:, None]

    def to_groups(input_array):
        return input_array.reshape(SLICE_LENGTH, KEY_VALUE_HEADS, query_group_width, HEAD_WIDTH).transpose(1, 2, 0, 3).reshape(KEY_VALUE_HEADS, query_group_width * SLICE_LENGTH, HEAD_WIDTH)

    def one_sample(carry, inputs):
        query, output, grad, saved_log_norms, length, slice_key_head, slice_value_head = inputs
        q_rows = to_groups(query)
        o_rows = to_groups(output)
        live_rows = row_pos < length
        g_rows = jnp.where(live_rows[None, :, None], to_groups(grad), jnp.zeros((), jnp.bfloat16))
        per_row_norms = saved_log_norms.reshape(KEY_VALUE_HEADS, query_group_width * SLICE_LENGTH)
        slice_keys = divide_heads(slice_key_head, KEY_VALUE_HEADS)
        slice_values = divide_heads(slice_value_head, KEY_VALUE_HEADS)

        def one_head(call_arguments):
            query_head, output_head, output_grad_head, head_log_norm, prompt_key_head, prompt_value_head, slice_key_single, slice_value_single = call_arguments
            row_delta = lax.optimization_barrier(jnp.sum(output_grad_head.astype(jnp.float32) * output_head.astype(jnp.float32), axis=-1))

            def partial_terms(keys, values, mask):
                scores = jnp.dot(query_head, keys.T, preferred_element_type=jnp.float32) * score_scale
                prob_rows = jnp.exp(scores - head_log_norm[:, None])
                if mask is not None:
                    prob_rows = jnp.where(mask, prob_rows, 0.0)
                dprobs = jnp.dot(output_grad_head, values.T, preferred_element_type=jnp.float32)
                score_grads = (prob_rows * (dprobs - row_delta[:, None])).astype(jnp.bfloat16)
                prob_low = prob_rows.astype(jnp.bfloat16)
                query_grad = jnp.dot(score_grads, keys, preferred_element_type=jnp.float32) * score_scale
                key_grad = jnp.dot(score_grads.T, query_head, preferred_element_type=jnp.float32) * score_scale
                value_grad = jnp.dot(prob_low.T, output_grad_head, preferred_element_type=jnp.float32)
                return (query_grad, key_grad, value_grad)
            query_prompt, key_prompt, value_prompt = partial_terms(prompt_key_head, prompt_value_head, None)
            slice_query_rows, slice_key_gradient, slice_value_gradient = partial_terms(slice_key_single, slice_value_single, visible_mask)
            return (query_prompt + slice_query_rows, key_prompt, value_prompt, slice_key_gradient, slice_value_gradient)
        query_rows_every, key_prompt, value_prompt, slice_key_gradient, slice_value_gradient = lax.map(one_head, (q_rows, o_rows, g_rows, per_row_norms, expanded_key_heads, expanded_value_heads, slice_keys, slice_values))
        flattened_query = query_rows_every.reshape(KEY_VALUE_HEADS, query_group_width, SLICE_LENGTH, HEAD_WIDTH).transpose(2, 0, 1, 3).reshape(SLICE_LENGTH, QUERY_HEADS * HEAD_WIDTH)
        new_carry = (carry[0] + join_heads(key_prompt), carry[1] + join_heads(value_prompt))
        return (new_carry, (flattened_query.astype(jnp.bfloat16), join_heads(slice_key_gradient).astype(jnp.bfloat16), join_heads(slice_value_gradient).astype(jnp.bfloat16)))
    starting_state = (jnp.zeros((PROMPT_LENGTH, KEY_VALUE_HEADS * HEAD_WIDTH), jnp.float32), jnp.zeros((PROMPT_LENGTH, KEY_VALUE_HEADS * HEAD_WIDTH), jnp.float32))
    sums, stacked = lax.scan(one_sample, starting_state, (queries, outputs, grad_out, log_norms, lengths, slice_key_rows, slice_value_rows))
    return (stacked[0], sums[0].astype(jnp.bfloat16), sums[1].astype(jnp.bfloat16), stacked[1], stacked[2])
```

```python
import functools
import math

import jax
import jax.numpy as jnp
from jax import lax
from jax.experimental import pallas as pl
from jax.experimental.pallas import tpu as pltpu
from jax.sharding import PartitionSpec as P

HEAD_WIDTH = 128
MESH = pl.DeviceIdType.MESH
LOG2E = 1.4426950408889634
F32 = jnp.float32
BF16 = jnp.bfloat16


def dot_nt(a, b):
    return lax.dot_general(a, b, (((1,), (1,)), ((), ())), preferred_element_type=F32)


def dot_nn(a, b):
    return lax.dot_general(a, b, (((1,), (0,)), ((), ())), preferred_element_type=F32)


def dot_tn(a, b):
    return lax.dot_general(a, b, (((0,), (0,)), ((), ())), preferred_element_type=F32)


def kernel(
    n_col, n_span, kv, group,
    len_ref, q_ref, o_ref, g_ref, lse_ref, pk_ref, pv_ref, sk_ref, sv_ref,
    dq_ref, dkp_ref, dvp_ref, dks_ref, dvs_ref,
    qst, gst, lse2, delta, kv_all, probs, grads, dqt, dqf, dqs, dqr,
    own, ysend, yrecv, zsend, zrecv,
    kv_recv, kvz_send, kvy_send, y_ssem, y_rsem, z_ssem, z_rsem, q_ssem, q_rsem,
):
    rows = q_ref.shape[1]
    shard = pk_ref.shape[0]
    width = HEAD_WIDTH
    part = rows // n_span
    scale = 1.0 / math.sqrt(HEAD_WIDTH)
    sample = lax.axis_index("sample")
    span = lax.axis_index("span")
    core = lax.axis_index("kvhead")
    col = sample // 2
    side = sample % 2

    def at_sample(c, y):
        return (c * 2 + y, span, core)

    def column(k):
        return lax.rem(col - k + n_col, n_col)

    partner = at_sample(col, 1 - side)

    barrier = pltpu.get_barrier_semaphore()
    for d in range(1, n_col):
        pl.semaphore_signal(barrier, inc=1, device_id=at_sample(column(d), side), device_id_type=MESH)
    pl.semaphore_signal(barrier, inc=1, device_id=partner, device_id_type=MESH)
    for e in range(1, n_span):
        peer = (sample, lax.rem(span + e, n_span), core)
        pl.semaphore_signal(barrier, inc=1, device_id=peer, device_id_type=MESH)

    for g in range(kv):
        lanes = slice(g * width, (g + 1) * width)
        kv_all[g, sample, :, 0:width] = pk_ref[:, lanes]
        kv_all[g, sample, :, width:2 * width] = pv_ref[:, lanes]
    pl.semaphore_wait(barrier, n_col + n_span - 1)

    def z_copy(g, d):
        return pltpu.make_async_remote_copy(
            src_ref=kv_all.at[g, sample], dst_ref=kv_all.at[g, sample],
            send_sem=kvz_send.at[g, d], recv_sem=kv_recv.at[g, sample],
            device_id=at_sample(lax.rem(col + d, n_col), side), device_id_type=MESH)

    def y_copy(g, k):
        s = column(k) * 2 + side
        return pltpu.make_async_remote_copy(
            src_ref=kv_all.at[g, s], dst_ref=kv_all.at[g, s],
            send_sem=kvy_send.at[g, k], recv_sem=kv_recv.at[g, s],
            device_id=partner, device_id_type=MESH)

    def wait_block(g, s):
        pltpu.make_async_remote_copy(
            src_ref=kv_all.at[g, s], dst_ref=kv_all.at[g, s],
            send_sem=kvy_send.at[g, 0], recv_sem=kv_recv.at[g, s],
            device_id=partner, device_id_type=MESH).wait_recv()

    def forward(g, k):
        wait_block(g, column(k) * 2 + side)
        y_copy(g, k).start()

    def ysum_copy(g, k):
        return pltpu.make_async_remote_copy(
            src_ref=ysend.at[g, k], dst_ref=yrecv.at[g, k],
            send_sem=y_ssem.at[g, k], recv_sem=y_rsem.at[g, k],
            device_id=partner, device_id_type=MESH)

    def zsum_copy(g, k):
        return pltpu.make_async_remote_copy(
            src_ref=zsend.at[g, k], dst_ref=zrecv.at[g, k],
            send_sem=z_ssem.at[g, k], recv_sem=z_rsem.at[g, k],
            device_id=at_sample(column(k), side), device_id_type=MESH)

    def query_copy(g, e):
        other = lax.rem(span + e, n_span)
        return pltpu.make_async_remote_copy(
            src_ref=dqs.at[g, other], dst_ref=dqr.at[g, e],
            send_sem=q_ssem.at[g, e], recv_sem=q_rsem.at[g, e],
            device_id=(sample, other, core), device_id_type=MESH)

    for g in range(kv):
        for d in range(1, n_col):
            z_copy(g, d).start()
        y_copy(g, 0).start()

    live = lax.broadcasted_iota(jnp.int32, (rows, width), 0) < len_ref[0]
    lse2[...] = lse_ref[0] * LOG2E
    for h in range(kv * group):
        lanes = slice(h * width, (h + 1) * width)
        g, i = divmod(h, group)
        span_rows = slice(i * rows, (i + 1) * rows)
        qst[g, span_rows, :] = q_ref[0, :, lanes]
        grad = jnp.where(live, g_ref[0, :, lanes].astype(F32), 0.0)
        gst[g, span_rows, :] = grad.astype(BF16)
        prod = grad * o_ref[0, :, lanes].astype(F32)
        delta[h:h + 1, :] = jnp.sum(prod.T, axis=0, keepdims=True)

    def block(g, keys, values, mask, first):
        count = keys.shape[0]
        for i in range(group):
            h = g * group + i
            span_rows = slice(i * rows, (i + 1) * rows)
            scores = dot_nt(keys, qst[g, span_rows, :])
            prob = jnp.exp2(scores * (scale * LOG2E) - lse2[h:h + 1, :])
            if mask is not None:
                prob = jnp.where(mask, prob, 0.0)
            dprob = dot_nt(values, gst[g, span_rows, :])
            probs[0:count, span_rows] = prob.astype(BF16)
            grads[0:count, span_rows] = (prob * (dprob - delta[h:h + 1, :])).astype(BF16)
        low = grads[0:count, :]
        term = dot_tn(keys, low)
        if first:
            dqt[...] = term
        else:
            dqt[...] += term
        key_grad = dot_nn(low, qst[g]) * scale
        value_grad = dot_nn(probs[0:count, :], gst[g])
        return key_grad, value_grad

    self_rows = sk_ref.shape[1]
    key_pos = span * self_rows + lax.broadcasted_iota(jnp.int32, (self_rows, rows), 0)
    visible = key_pos <= lax.broadcasted_iota(jnp.int32, (self_rows, rows), 1)

    def column_block(g, k):
        c = column(k)
        pair = kv_all[g, pl.ds(c * 2, 2)].reshape(2 * shard, 2 * width)
        key_grad, value_grad = block(g, pair[:, :width], pair[:, width:], None, False)
        own[0, :, 0:width] = key_grad[:shard]
        own[1, :, 0:width] = key_grad[shard:]
        own[0, :, width:] = value_grad[:shard]
        own[1, :, width:] = value_grad[shard:]
        ysend[g, k] = own[1 - side].astype(BF16)
        ysum_copy(g, k).start()
        dqf_own = own[side]
        return dqf_own

    def z_finish(g, k):
        ysum_copy(g, k).wait_recv()
        zsend[g, k] = (zhold[g, k] + yrecv[g, k].astype(F32)).astype(BF16)
        zsum_copy(g, k).start()

    zhold = dqf["hold"]
    dq_acc = dqf["query"]

    for g in range(kv):
        lanes = slice(g * width, (g + 1) * width)
        key_grad, value_grad = block(g, sk_ref[0, :, lanes], sv_ref[0, :, lanes], visible, True)
        dks_ref[0, :, lanes] = key_grad.astype(BF16)
        dvs_ref[0, :, lanes] = value_grad.astype(BF16)
        if g == 0:
            forward(g, 1)

        def step(k, carry, g=g):
            if g == 0:
                @pl.when(k + 1 < n_col)
                def _():
                    forward(g, k + 1)
            wait_block(g, column(k) * 2 + 1 - side)
            zhold[g, k] = column_block(g, k)

            @pl.when(k >= 2)
            def _():
                z_finish(g, k - 1)
            return carry

        lax.fori_loop(1, n_col, step, 0)
        for later in range(1, kv):
            if g == 0:
                for k in range(1, n_col):
                    forward(later, k)
        wait_block(g, column(0) * 2 + 1 - side)
        zhold[g, 0] = column_block(g, 0)
        z_finish(g, n_col - 1)
        for i in range(group):
            lanes_i = slice(i * width, (i + 1) * width)
            part_sum = dqt[:, i * rows:(i + 1) * rows].T * scale
            whole = part_sum.reshape(n_span, part, width)
            dq_acc[g, :, :, lanes_i] = whole
            dqs[g, :, :, lanes_i] = whole.astype(BF16)
        for e in range(1, n_span):
            query_copy(g, e).start()

    for g in range(kv):
        lanes = slice(g * width, (g + 1) * width)
        ysum_copy(g, 0).wait_recv()
        total = zhold[g, 0] + yrecv[g, 0].astype(F32)
        for k in range(1, n_col):
            zsum_copy(g, k).wait_recv()
            total += zrecv[g, k].astype(F32)
        dkp_ref[:, lanes] = total[:, :width].astype(BF16)
        dvp_ref[:, lanes] = total[:, width:].astype(BF16)
        query_total = dq_acc[g, span]
        for e in range(1, n_span):
            query_copy(g, e).wait_recv()
            query_total += dqr[g, e].astype(F32)
        dq_ref[0, :, g * group * width:(g + 1) * group * width] = query_total.astype(BF16)

    for g in range(kv):
        for d in range(1, n_col):
            z_copy(g, d).wait_send()
            zsum_copy(g, d).wait_send()
        for k in range(n_col):
            y_copy(g, k).wait_send()
            ysum_copy(g, k).wait_send()
        for e in range(1, n_span):
            query_copy(g, e).wait_send()


def body(n_col, n_span, kv, group, *refs):
    refs = list(refs)
    fixed = refs[:14]
    (qst, gst, lse2, delta, kv_all, probs, grads, dqt, query, hold) = refs[14:24]
    rest = refs[24:]
    kernel(n_col, n_span, kv, group, *fixed, qst, gst, lse2, delta, kv_all, probs, grads, dqt,
           {"query": query, "hold": hold}, *rest)


def shards(n_sample, n_span, queries, outputs, grad_out, log_norms, lengths,
           prompt_key_rows, prompt_value_rows, slice_key_rows, slice_value_rows):
    rows = queries.shape[1]
    shard = prompt_key_rows.shape[0]
    width = HEAD_WIDTH
    kv = prompt_key_rows.shape[1] // width
    heads = queries.shape[2] // width
    group = heads // kv
    n_col = n_sample // 2
    part = rows // n_span
    vmem = pl.BlockSpec(memory_space=pltpu.VMEM)
    dma = pltpu.SemaphoreType.DMA
    out_shape = (
        jax.ShapeDtypeStruct((1, part, heads * width), BF16),
        jax.ShapeDtypeStruct(prompt_key_rows.shape, BF16),
        jax.ShapeDtypeStruct(prompt_key_rows.shape, BF16),
        jax.ShapeDtypeStruct(slice_key_rows.shape, BF16),
        jax.ShapeDtypeStruct(slice_key_rows.shape, BF16),
    )
    scratch = [
        pltpu.VMEM((kv, group * rows, width), BF16),
        pltpu.VMEM((kv, group * rows, width), BF16),
        pltpu.VMEM((heads, rows), F32),
        pltpu.VMEM((heads, rows), F32),
        pltpu.VMEM((kv, n_sample, shard, 2 * width), BF16),
        pltpu.VMEM((2 * shard, group * rows), BF16),
        pltpu.VMEM((2 * shard, group * rows), BF16),
        pltpu.VMEM((width, group * rows), F32),
        pltpu.VMEM((kv, n_span, part, group * width), F32),
        pltpu.VMEM((kv, n_col, shard, 2 * width), F32),
        pltpu.VMEM((kv, n_span, part, group * width), BF16),
        pltpu.VMEM((kv, n_span, part, group * width), BF16),
        pltpu.VMEM((2, shard, 2 * width), F32),
        pltpu.VMEM((kv, n_col, shard, 2 * width), BF16),
        pltpu.VMEM((kv, n_col, shard, 2 * width), BF16),
        pltpu.VMEM((kv, n_col, shard, 2 * width), BF16),
        pltpu.VMEM((kv, n_col, shard, 2 * width), BF16),
        dma((kv, n_sample)), dma((kv, n_col)), dma((kv, n_col)),
        dma((kv, n_col)), dma((kv, n_col)), dma((kv, n_col)), dma((kv, n_col)),
        dma((kv, n_span)), dma((kv, n_span)),
    ]
    return pl.pallas_call(
        functools.partial(body, n_col, n_span, kv, group),
        out_shape=out_shape,
        in_specs=[pl.BlockSpec(memory_space=pltpu.SMEM)] + [vmem] * 8,
        out_specs=(vmem,) * 5,
        scratch_shapes=scratch,
        compiler_params=pltpu.CompilerParams(
            collective_id=0, has_side_effects=True, vmem_limit_bytes=48 * 1024 * 1024),
        cost_estimate=pl.CostEstimate(
            flops=10 * heads * rows * (n_sample * shard + slice_key_rows.shape[1]) * width,
            bytes_accessed=8 * 1024 * 1024, transcendentals=heads * rows * n_sample * shard),
    )(lengths, queries, outputs, grad_out, log_norms,
      prompt_key_rows, prompt_value_rows, slice_key_rows, slice_value_rows)


def solution(mesh):
    in_specs = (
        P("sample", None, "kvhead"),
        P("sample", None, "kvhead"),
        P("sample", None, "kvhead"),
        P("sample", "kvhead", None),
        P("sample"),
        P(("sample", "span"), "kvhead"),
        P(("sample", "span"), "kvhead"),
        P("sample", "span", "kvhead"),
        P("sample", "span", "kvhead"),
    )
    out_specs = (
        P("sample", "span", "kvhead"),
        P(("sample", "span"), "kvhead"),
        P(("sample", "span"), "kvhead"),
        P("sample", "span", "kvhead"),
        P("sample", "span", "kvhead"),
    )
    return jax.shard_map(
        functools.partial(shards, mesh.shape["sample"], mesh.shape["span"]),
        mesh=mesh, in_specs=in_specs, out_specs=out_specs, check_vma=False)
```

```python
import functools
import math

import jax
import jax.numpy as jnp
from jax import lax
from jax.experimental import pallas as pl
from jax.experimental.pallas import tpu as pltpu
from jax.sharding import PartitionSpec as P

HEAD_WIDTH = 128
MESH = pl.DeviceIdType.MESH
LOG2E = 1.4426950408889634
F32 = jnp.float32
BF16 = jnp.bfloat16


def dot_nt(a, b):
    return lax.dot_general(a, b, (((1,), (1,)), ((), ())), preferred_element_type=F32)


def dot_nn(a, b):
    return lax.dot_general(a, b, (((1,), (0,)), ((), ())), preferred_element_type=F32)


def dot_tn(a, b):
    return lax.dot_general(a, b, (((0,), (0,)), ((), ())), preferred_element_type=F32)


def kernel(
    n_col, n_span, kv, group,
    len_ref, q_hbm, o_hbm, g_hbm, lse_hbm, pk_hbm, pv_hbm, sk_hbm, sv_hbm,
    dq_ref, dkp_ref, dvp_ref, dks_ref, dvs_ref,
    qst, gst, lse2, delta, kv_all, probs, grads, dqt, dqf, dqs, dqr,
    own, ysend, yrecv, zsend, zrecv,
    q_ref, o_ref, g_ref, lse_ref, sk_ref, sv_ref, load_sem,
    kv_recv, kvz_send, kvy_send, y_ssem, y_rsem, z_ssem, z_rsem, q_ssem, q_rsem,
):
    rows = q_hbm.shape[1]
    shard = pk_hbm.shape[0]
    width = HEAD_WIDTH
    part = rows // n_span
    scale = 1.0 / math.sqrt(HEAD_WIDTH)
    sample = lax.axis_index("sample")
    span = lax.axis_index("span")
    core = lax.axis_index("kvhead")
    col = sample // 2
    side = sample % 2

    def at_sample(c, y):
        return (c * 2 + y, span, core)

    def column(k):
        return lax.rem(col - k + n_col, n_col)

    partner = at_sample(col, 1 - side)

    loads = []
    for g in range(kv):
        lanes = slice(g * width, (g + 1) * width)
        for n, source in enumerate((pk_hbm, pv_hbm)):
            target = kv_all.at[g, sample, :, n * width:(n + 1) * width]
            loads.append(pltpu.make_async_copy(source.at[:, lanes], target, load_sem.at[len(loads)]))
    for source, target in ((q_hbm, q_ref), (g_hbm, g_ref), (o_hbm, o_ref), (lse_hbm, lse_ref),
                           (sk_hbm, sk_ref), (sv_hbm, sv_ref)):
        loads.append(pltpu.make_async_copy(source, target, load_sem.at[len(loads)]))

    barrier = pltpu.get_barrier_semaphore()
    for d in range(1, n_col):
        pl.semaphore_signal(barrier, inc=1, device_id=at_sample(column(d), side), device_id_type=MESH)
    pl.semaphore_signal(barrier, inc=1, device_id=partner, device_id_type=MESH)
    for e in range(1, n_span):
        peer = (sample, lax.rem(span + e, n_span), core)
        pl.semaphore_signal(barrier, inc=1, device_id=peer, device_id_type=MESH)

    for load in loads:
        load.start()
    for load in loads[:2 * kv]:
        load.wait()
    pl.semaphore_wait(barrier, n_col + n_span - 1)

    def z_copy(g, d):
        return pltpu.make_async_remote_copy(
            src_ref=kv_all.at[g, sample], dst_ref=kv_all.at[g, sample],
            send_sem=kvz_send.at[g, d], recv_sem=kv_recv.at[g, sample],
            device_id=at_sample(lax.rem(col + d, n_col), side), device_id_type=MESH)

    def y_copy(g, k):
        s = column(k) * 2 + side
        return pltpu.make_async_remote_copy(
            src_ref=kv_all.at[g, s], dst_ref=kv_all.at[g, s],
            send_sem=kvy_send.at[g, k], recv_sem=kv_recv.at[g, s],
            device_id=partner, device_id_type=MESH)

    def wait_block(g, s):
        pltpu.make_async_remote_copy(
            src_ref=kv_all.at[g, s], dst_ref=kv_all.at[g, s],
            send_sem=kvy_send.at[g, 0], recv_sem=kv_recv.at[g, s],
            device_id=partner, device_id_type=MESH).wait_recv()

    def forward(g, k):
        wait_block(g, column(k) * 2 + side)
        y_copy(g, k).start()

    def ysum_copy(g, k):
        return pltpu.make_async_remote_copy(
            src_ref=ysend.at[g, k], dst_ref=yrecv.at[g, k],
            send_sem=y_ssem.at[g, k], recv_sem=y_rsem.at[g, k],
            device_id=partner, device_id_type=MESH)

    def zsum_copy(g, k):
        return pltpu.make_async_remote_copy(
            src_ref=zsend.at[g, k], dst_ref=zrecv.at[g, k],
            send_sem=z_ssem.at[g, k], recv_sem=z_rsem.at[g, k],
            device_id=at_sample(column(k), side), device_id_type=MESH)

    def query_copy(g, e):
        other = lax.rem(span + e, n_span)
        return pltpu.make_async_remote_copy(
            src_ref=dqs.at[g, other], dst_ref=dqr.at[g, e],
            send_sem=q_ssem.at[g, e], recv_sem=q_rsem.at[g, e],
            device_id=(sample, other, core), device_id_type=MESH)

    for g in range(kv):
        for d in range(1, n_col):
            z_copy(g, d).start()
        y_copy(g, 0).start()

    for load in loads[2 * kv:]:
        load.wait()
    live = lax.broadcasted_iota(jnp.int32, (rows, width), 0) < len_ref[0]
    for h in range(kv * group):
        lanes = slice(h * width, (h + 1) * width)
        g, i = divmod(h, group)
        span_rows = slice(i * rows, (i + 1) * rows)
        qst[g, span_rows, :] = q_ref[0, :, lanes]
        grad = jnp.where(live, g_ref[0, :, lanes].astype(F32), 0.0)
        gst[g, span_rows, :] = grad.astype(BF16)
        prod = grad * o_ref[0, :, lanes].astype(F32)
        lse2[h:h + 1, :] = lse_ref[h] * LOG2E
        delta[h:h + 1, :] = jnp.sum(prod.T, axis=0, keepdims=True)

    def block(g, keys, values, mask, first):
        count = keys.shape[0]
        for i in range(group):
            h = g * group + i
            span_rows = slice(i * rows, (i + 1) * rows)
            scores = dot_nt(keys, qst[g, span_rows, :])
            prob = jnp.exp2(scores * (scale * LOG2E) - lse2[h:h + 1, :])
            if mask is not None:
                prob = jnp.where(mask, prob, 0.0)
            dprob = dot_nt(values, gst[g, span_rows, :])
            probs[0:count, span_rows] = prob.astype(BF16)
            grads[0:count, span_rows] = (prob * (dprob - delta[h:h + 1, :])).astype(BF16)
        low = grads[0:count, :]
        term = dot_tn(keys, low)
        if first:
            dqt[g] = term
        else:
            dqt[g] += term
        key_grad = dot_nn(low, qst[g]) * scale
        value_grad = dot_nn(probs[0:count, :], gst[g])
        return key_grad, value_grad

    self_rows = sk_ref.shape[1]
    key_pos = span * self_rows + lax.broadcasted_iota(jnp.int32, (self_rows, rows), 0)
    visible = key_pos <= lax.broadcasted_iota(jnp.int32, (self_rows, rows), 1)

    def column_block(g, k):
        c = column(k)
        pair = kv_all[g, pl.ds(c * 2, 2)].reshape(2 * shard, 2 * width)
        key_grad, value_grad = block(g, pair[:, :width], pair[:, width:], None, False)
        own[0, :, 0:width] = key_grad[:shard]
        own[1, :, 0:width] = key_grad[shard:]
        own[0, :, width:] = value_grad[:shard]
        own[1, :, width:] = value_grad[shard:]
        ysend[g, k] = own[1 - side].astype(BF16)
        ysum_copy(g, k).start()
        dqf_own = own[side]
        return dqf_own

    def z_finish(g, k):
        ysum_copy(g, k).wait_recv()
        zsend[g, k] = (zhold[g, k] + yrecv[g, k].astype(F32)).astype(BF16)
        zsum_copy(g, k).start()

    zhold = dqf["hold"]
    dq_acc = dqf["query"]

    for g in range(kv):
        lanes = slice(g * width, (g + 1) * width)
        key_grad, value_grad = block(g, sk_ref[0, :, lanes], sv_ref[0, :, lanes], visible, True)
        dks_ref[0, :, lanes] = key_grad.astype(BF16)
        dvs_ref[0, :, lanes] = value_grad.astype(BF16)
        for k in range(1, n_col):
            forward(g, k)

    for g in range(kv):
        def step(k, carry, g=g):
            wait_block(g, column(k) * 2 + 1 - side)
            zhold[g, k] = column_block(g, k)

            @pl.when(k >= 3)
            def _():
                z_finish(g, k - 2)
            return carry

        lax.fori_loop(1, n_col, step, 0)
        wait_block(g, column(0) * 2 + 1 - side)
        zhold[g, 0] = column_block(g, 0)
        for i in range(group):
            lanes_i = slice(i * width, (i + 1) * width)
            part_sum = dqt[g, :, i * rows:(i + 1) * rows].T * scale
            whole = part_sum.reshape(n_span, part, width)
            dq_acc[g, :, :, lanes_i] = whole
            dqs[g, :, :, lanes_i] = whole.astype(BF16)
        for e in range(1, n_span):
            query_copy(g, e).start()
        for k in range(max(1, n_col - 2), n_col):
            z_finish(g, k)

    for g in range(kv):
        lanes = slice(g * width, (g + 1) * width)
        ysum_copy(g, 0).wait_recv()
        total = zhold[g, 0] + yrecv[g, 0].astype(F32)
        for k in range(1, n_col):
            zsum_copy(g, k).wait_recv()
            total += zrecv[g, k].astype(F32)
        dkp_ref[:, lanes] = total[:, :width].astype(BF16)
        dvp_ref[:, lanes] = total[:, width:].astype(BF16)
        query_total = dq_acc[g, span]
        for e in range(1, n_span):
            query_copy(g, e).wait_recv()
            query_total += dqr[g, e].astype(F32)
        dq_ref[0, :, g * group * width:(g + 1) * group * width] = query_total.astype(BF16)

    for g in range(kv):
        for d in range(1, n_col):
            z_copy(g, d).wait_send()
            zsum_copy(g, d).wait_send()
        for k in range(n_col):
            y_copy(g, k).wait_send()
            ysum_copy(g, k).wait_send()
        for e in range(1, n_span):
            query_copy(g, e).wait_send()


def body(n_col, n_span, kv, group, *refs):
    refs = list(refs)
    fixed = refs[:14]
    (qst, gst, lse2, delta, kv_all, probs, grads, dqt, query, hold) = refs[14:24]
    rest = refs[24:]
    kernel(n_col, n_span, kv, group, *fixed, qst, gst, lse2, delta, kv_all, probs, grads, dqt,
           {"query": query, "hold": hold}, *rest)


def shards(n_sample, n_span, queries, outputs, grad_out, log_norms, lengths,
           prompt_key_rows, prompt_value_rows, slice_key_rows, slice_value_rows):
    rows = queries.shape[1]
    shard = prompt_key_rows.shape[0]
    width = HEAD_WIDTH
    kv = prompt_key_rows.shape[1] // width
    heads = queries.shape[2] // width
    group = heads // kv
    n_col = n_sample // 2
    part = rows // n_span
    vmem = pl.BlockSpec(memory_space=pltpu.VMEM)
    dma = pltpu.SemaphoreType.DMA
    out_shape = (
        jax.ShapeDtypeStruct((1, part, heads * width), BF16),
        jax.ShapeDtypeStruct(prompt_key_rows.shape, BF16),
        jax.ShapeDtypeStruct(prompt_key_rows.shape, BF16),
        jax.ShapeDtypeStruct(slice_key_rows.shape, BF16),
        jax.ShapeDtypeStruct(slice_key_rows.shape, BF16),
    )
    scratch = [
        pltpu.VMEM((kv, group * rows, width), BF16),
        pltpu.VMEM((kv, group * rows, width), BF16),
        pltpu.VMEM((heads, rows), F32),
        pltpu.VMEM((heads, rows), F32),
        pltpu.VMEM((kv, n_sample, shard, 2 * width), BF16),
        pltpu.VMEM((2 * shard, group * rows), BF16),
        pltpu.VMEM((2 * shard, group * rows), BF16),
        pltpu.VMEM((kv, width, group * rows), F32),
        pltpu.VMEM((kv, n_span, part, group * width), F32),
        pltpu.VMEM((kv, n_col, shard, 2 * width), F32),
        pltpu.VMEM((kv, n_span, part, group * width), BF16),
        pltpu.VMEM((kv, n_span, part, group * width), BF16),
        pltpu.VMEM((2, shard, 2 * width), F32),
        pltpu.VMEM((kv, n_col, shard, 2 * width), BF16),
        pltpu.VMEM((kv, n_col, shard, 2 * width), BF16),
        pltpu.VMEM((kv, n_col, shard, 2 * width), BF16),
        pltpu.VMEM((kv, n_col, shard, 2 * width), BF16),
        pltpu.VMEM(queries.shape, BF16),
        pltpu.VMEM(queries.shape, BF16),
        pltpu.VMEM(queries.shape, BF16),
        pltpu.VMEM((heads, 1, rows), F32),
        pltpu.VMEM(slice_key_rows.shape, BF16),
        pltpu.VMEM(slice_key_rows.shape, BF16),
        dma((2 * kv + 6,)),
        dma((kv, n_sample)), dma((kv, n_col)), dma((kv, n_col)),
        dma((kv, n_col)), dma((kv, n_col)), dma((kv, n_col)), dma((kv, n_col)),
        dma((kv, n_span)), dma((kv, n_span)),
    ]
    return pl.pallas_call(
        functools.partial(body, n_col, n_span, kv, group),
        out_shape=out_shape,
        in_specs=[pl.BlockSpec(memory_space=pltpu.SMEM)] + [pl.BlockSpec(memory_space=pltpu.HBM)] * 8,
        out_specs=(vmem,) * 5,
        scratch_shapes=scratch,
        compiler_params=pltpu.CompilerParams(
            collective_id=0, has_side_effects=True, vmem_limit_bytes=60 * 1024 * 1024),
        cost_estimate=pl.CostEstimate(
            flops=10 * heads * rows * (n_sample * shard + slice_key_rows.shape[1]) * width,
            bytes_accessed=8 * 1024 * 1024, transcendentals=heads * rows * n_sample * shard),
    )(lengths, queries, outputs, grad_out, log_norms.reshape(heads, 1, rows),
      prompt_key_rows, prompt_value_rows, slice_key_rows, slice_value_rows)


def solution(mesh):
    in_specs = (
        P("sample", None, "kvhead"),
        P("sample", None, "kvhead"),
        P("sample", None, "kvhead"),
        P("sample", "kvhead", None),
        P("sample"),
        P(("sample", "span"), "kvhead"),
        P(("sample", "span"), "kvhead"),
        P("sample", "span", "kvhead"),
        P("sample", "span", "kvhead"),
    )
    out_specs = (
        P("sample", "span", "kvhead"),
        P(("sample", "span"), "kvhead"),
        P(("sample", "span"), "kvhead"),
        P("sample", "span", "kvhead"),
        P("sample", "span", "kvhead"),
    )
    return jax.shard_map(
        functools.partial(shards, mesh.shape["sample"], mesh.shape["span"]),
        mesh=mesh, in_specs=in_specs, out_specs=out_specs, check_vma=False)
```
